32 devices in a mesh: ctx: 4 (over z), head: 2 (over x), rep: 4 (over y, core).
Axes of the slice: x: 2, y: 2, z: 4, core: 2. Of those that a mesh axis runs over, the one named last changes fastest.
Arguments:
- queries: bfloat16 [4, 512, 8192], P('rep', 'ctx', 'head'), may hold values from -12 to 12
- keys: bfloat16 [4, 512, 1024], P('rep', 'ctx', 'head'), may hold values from -12 to 12
- values: bfloat16 [4, 512, 1024], P('rep', 'ctx', 'head'), may hold values from -6 to 6
- grad_out: bfloat16 [4, 512, 8192], P('rep', 'ctx', 'head'), may hold values from -90 to 90
- segment_ids: int32 [4, 512], P('rep'), may hold values from 0 to 7, never falling along the last dimension, each value on 1 to 256 neighbouring positions
- head_mask: float32 [64], P('head'), may hold values from 0.25 to 1
- ablated_heads: int32 [8], replicated, may hold values from 0 to 63, as said below
- w_query: bfloat16 [8192, 8192], P(('ctx', 'rep'), 'head'), may hold values from -0.0625 to 0.0625
- w_key: bfloat16 [8192, 1024], P(('ctx', 'rep'), 'head'), may hold values from -0.0625 to 0.0625
- w_value: bfloat16 [8192, 1024], P(('ctx', 'rep'), 'head'), may hold values from -0.0625 to 0.0625
Outputs:
- input_grad: bfloat16 [4, 512, 8192], P('rep', None, ('ctx', 'head'))
- mask_grad: float32 [64], P('head')
The draws below stay inside these ranges and needn't reach their ends.
Inputs may be any that keep to these rules, and one draw needn't show every extreme that they name: `ablated_heads`: the 8 entries are all different.
All inputs are finite; a program needn't handle non-finite values.
Results may differ from the reference program's by a relative error of at most 0.02.
Values may be sent and summed in bfloat16 or wider, within the bound.
A program may use at most 192 MiB of HBM per device.

```python
import math
import jax
import jax.numpy as jnp
import numpy as np
from jax import lax

D = 8192
HEADS = 64
KVH = 8
DH = 128
TOK_DEV = 128
NABL = 8
SEQ = 512
REPS = 4
DOCS = 8
N_HEAD = 2


def draw_queries(key, part):
    shape = (REPS, SEQ, HEADS, DH)
    noise = jnp.clip(jax.random.normal(jax.random.fold_in(key, 1), shape), -6.0, 6.0)
    factor = jnp.exp(jax.random.uniform(jax.random.fold_in(key, 2), (REPS, SEQ, HEADS, 1), minval=math.log(0.6), maxval=math.log(2.0)))
    drawn = noise * factor
    return drawn.reshape(REPS, SEQ, HEADS * DH).astype(jnp.bfloat16)


def draw_keys(key, part):
    shape = (REPS, SEQ, KVH, DH)
    noise = jnp.clip(jax.random.normal(jax.random.fold_in(key, 3), shape), -6.0, 6.0)
    factor = jnp.exp(jax.random.uniform(jax.random.fold_in(key, 4), (REPS, SEQ, KVH, 1), minval=math.log(0.6), maxval=math.log(2.0)))
    drawn = noise * factor
    return drawn.reshape(REPS, SEQ, KVH * DH).astype(jnp.bfloat16)


def draw_grad_out(key, part):
    shape = (REPS, SEQ, HEADS * DH)
    blocks_total = SEQ // TOK_DEV
    place = jnp.arange(SEQ, dtype=jnp.float32)[None, :, None] / SEQ + jnp.arange(REPS, dtype=jnp.float32)[:, None, None] / (REPS * blocks_total)
    noise = jnp.clip(jax.random.normal(jax.random.fold_in(key, 5), shape), -6.0, 6.0)
    rising = jnp.exp(math.log(3.0) * place)
    return (2.0 * noise * rising).astype(jnp.bfloat16)


def draw_ablated_heads(key, part):
    others = jax.random.permutation(jax.random.fold_in(key, 7), HEADS - 1)[:NABL - 1].astype(jnp.int32)
    listed = jnp.concatenate([others, jnp.full((1,), HEADS - 1, jnp.int32)])
    return jax.random.permutation(jax.random.fold_in(key, 8), listed).astype(jnp.int32)


def block_levels(own_key, extent, pieces, low, top_value):
    def one(position, blocks):
        draws = jax.random.uniform(jax.random.fold_in(jax.random.fold_in(own_key, 6), position), (blocks,), jnp.float32, low / len(pieces), top_value / len(pieces))
        return jnp.repeat(jnp.exp(draws), extent[position] // blocks).reshape((-1,) + (1,) * (len(extent) - position - 1))

    factor_of = one(*pieces[0])
    for cut in pieces[1:]:
        factor_of = factor_of * one(*cut)
    return factor_of


def profile(count, total, reach, slope):
    weights = [(1 << 20) // math.isqrt(standing ** slope) + 1 for standing in range(2, count + 1)]
    rest, counts = total - reach - (count - 1), [1] * (count - 1)
    while rest > 0:
        candidates = [i for i in range(count - 1) if counts[i] < reach]
        whole, remaining = sum([weights[i] for i in candidates]), rest
        for i in candidates:
            extra = min(reach - counts[i], max(1, remaining * weights[i] // whole), rest)
            counts[i] = counts[i] + extra
            rest = rest - extra
    return np.array([reach] + counts)


def uneven(rng, count, total, most, skew):
    if count == 2:
        one = jax.random.randint(rng, (), max(1, total - most), min(most, total - 1) + 1)
        return jnp.stack([one, total - one])
    sizes = jnp.asarray(profile(count, total, most, skew), jnp.int32)
    twos = (count - 1) // 2
    source_of, sink = sizes[1:1 + 2 * twos:2], sizes[2:2 + 2 * twos:2]
    slack = jnp.minimum(source_of - 1, most - sink)
    passed = jax.random.randint(jax.random.fold_in(rng, 1), (twos,), 0, 1 << 20) % (slack + 1)
    sizes = sizes.at[1:1 + 2 * twos:2].set(source_of - passed).at[2:2 + 2 * twos:2].set(sink + passed)
    return sizes[jax.random.permutation(jax.random.fold_in(rng, 2), count)]


def bell_draw(own_key, shape, deviation, reach, cuts=(), held_as=jnp.bfloat16):
    level = block_levels(own_key, shape, cuts, -0.22, 0.18) if cuts else 1.0
    values = jax.random.normal(own_key, shape, jnp.float32) * deviation * level
    return jnp.minimum(jnp.maximum(values, -reach), reach).astype(held_as)


def setup_inputs(seed: int = 0) -> dict:
    key_list = jax.random.split(jax.random.key(seed), 11)
    return {
        "queries": draw_queries(jax.random.fold_in(key_list[10], 71), 0),
        "keys": draw_keys(jax.random.fold_in(key_list[10], 71), 0),
        "values": bell_draw(key_list[2], (REPS, SEQ, KVH * DH), 1.0, 6.0, ((0, 4), (1, 4), (2, 2))),
        "grad_out": draw_grad_out(jax.random.fold_in(key_list[10], 71), 0),
        "segment_ids": jax.vmap(lambda own: jnp.searchsorted(jnp.cumsum(uneven(own, DOCS, SEQ, SEQ // 2, 2)), jnp.arange(SEQ), side="right"))(jax.random.split(key_list[4], REPS)).reshape((REPS, SEQ)).astype(jnp.int32),
        "head_mask": jnp.clip(0.25 + 0.75 * jax.random.uniform(key_list[5], (HEADS,), jnp.float32) ** block_levels(key_list[5], (HEADS,), ((0, 2),), -0.2, 0.2), 0.25, 1.0),
        "ablated_heads": draw_ablated_heads(jax.random.fold_in(key_list[10], 71), 0),
        "w_query": bell_draw(key_list[7], (D, HEADS * DH), D ** -0.5, 0.0625, ((0, 16), (1, 2))),
        "w_key": bell_draw(key_list[8], (D, KVH * DH), D ** -0.5, 0.0625, ((0, 16), (1, 2))),
        "w_value": bell_draw(key_list[9], (D, KVH * DH), D ** -0.5, 0.0625, ((0, 16), (1, 2))),
    }


NEG_FILL = -1e+30

def rounded(arr_values):
    return lax.optimization_barrier(arr_values.astype(jnp.bfloat16)).astype(jnp.float32)

def group_terms(group_items, segments):
    query_group, key_group, value_group, grad_group, scale_group = group_items
    length = key_group.shape[0]
    places = jnp.arange(length, dtype=jnp.int32)
    allowed = (places[None, :] <= places[:, None]) & (segments[None, :] == segments[:, None])
    score_scale = 1.0 / math.sqrt(DH)
    query_full = query_group.astype(jnp.float32)
    key_full = key_group.astype(jnp.float32)
    value_full = value_group.astype(jnp.float32)
    scores = jnp.einsum('hic,kc->hik', query_full, key_full) * score_scale
    scores = jnp.where(allowed[None], scores, NEG_FILL)
    row_max = lax.optimization_barrier(jnp.max(scores, axis=-1, keepdims=True))
    exponent = jnp.where(allowed[None], jnp.exp(scores - row_max), 0.0)
    denominator = lax.optimization_barrier(jnp.sum(exponent, axis=-1, keepdims=True))
    log_total = row_max + jnp.log(denominator)
    head_out = (jnp.einsum('hik,kc->hic', rounded(exponent), value_full) / denominator).astype(jnp.bfloat16)
    out_full = head_out.astype(jnp.float32)
    grad_full = grad_group.astype(jnp.float32)
    out_grad = rounded(scale_group[:, None, None] * grad_full)
    out_dot = lax.optimization_barrier(jnp.sum(out_grad * out_full, axis=-1, keepdims=True))
    probability = jnp.where(allowed[None], jnp.exp(scores - log_total), 0.0)
    value_grad = jnp.einsum('hik,hic->kc', rounded(probability), out_grad).astype(jnp.bfloat16)
    prob_grad = jnp.einsum('hic,kc->hik', out_grad, value_full)
    score_grad = rounded(probability * (prob_grad - out_dot))
    query_grad = (jnp.einsum('hik,kc->hic', score_grad, key_full) * score_scale).astype(jnp.bfloat16)
    key_grad = (jnp.einsum('hik,hic->kc', score_grad, query_full) * score_scale).astype(jnp.bfloat16)
    mask_terms = lax.optimization_barrier(jnp.sum(out_full * grad_full, axis=(1, 2)))
    return (query_grad, key_grad, value_grad, mask_terms)

def reference(queries, keys, values, grad_out, segment_ids, head_mask, ablated_heads, w_query, w_key, w_value):
    per_group = HEADS // KVH
    head_ids = jnp.arange(HEADS, dtype=jnp.int32)
    ablate = jnp.any(head_ids[:, None] == ablated_heads[None, :], axis=1)
    head_scale = jnp.where(ablate, 0.0, head_mask).astype(jnp.float32).reshape(KVH, per_group)
    shard_groups = KVH // N_HEAD
    query_cols = shard_groups * per_group * DH
    pair_cols = shard_groups * DH

    def one_prompt(prompt_items):
        query_rows_in, key_rows_in, value_rows_in, grad_rows_in, segments = prompt_items
        query_blocks = query_rows_in.reshape(SEQ, KVH, per_group, DH).transpose(1, 2, 0, 3)
        grad_blocks = grad_rows_in.reshape(SEQ, KVH, per_group, DH).transpose(1, 2, 0, 3)
        key_blocks = key_rows_in.reshape(SEQ, KVH, DH).transpose(1, 0, 2)
        value_blocks = value_rows_in.reshape(SEQ, KVH, DH).transpose(1, 0, 2)
        query_grad, key_grad, value_grad, mask_terms = lax.map(lambda group_items: group_terms(group_items, segments), (query_blocks, key_blocks, value_blocks, grad_blocks, head_scale))
        query_rows = query_grad.transpose(2, 0, 1, 3).reshape(SEQ, HEADS * DH)
        key_rows = key_grad.transpose(1, 0, 2).reshape(SEQ, KVH * DH)
        value_rows = value_grad.transpose(1, 0, 2).reshape(SEQ, KVH * DH)

        def add_shard(carried, shard_index):
            start_query = shard_index * query_cols
            start_pair = shard_index * pair_cols
            product = jnp.dot(lax.dynamic_slice_in_dim(query_rows, start_query, query_cols, 1), lax.dynamic_slice_in_dim(w_query, start_query, query_cols, 1).T, preferred_element_type=jnp.float32)
            product = product + jnp.dot(lax.dynamic_slice_in_dim(key_rows, start_pair, pair_cols, 1), lax.dynamic_slice_in_dim(w_key, start_pair, pair_cols, 1).T, preferred_element_type=jnp.float32)
            product = product + jnp.dot(lax.dynamic_slice_in_dim(value_rows, start_pair, pair_cols, 1), lax.dynamic_slice_in_dim(w_value, start_pair, pair_cols, 1).T, preferred_element_type=jnp.float32)
            return (carried + rounded(product), None)
        summed_rows, unused = lax.scan(add_shard, jnp.zeros((SEQ, D), jnp.float32), jnp.arange(N_HEAD, dtype=jnp.int32))
        return (summed_rows.astype(jnp.bfloat16), mask_terms.reshape(HEADS))
    input_grad, prompt_terms = lax.map(one_prompt, (queries, keys, values, grad_out, segment_ids))
    mask_grad = lax.optimization_barrier(jnp.sum(prompt_terms, axis=0)) / math.sqrt(REPS * SEQ)
    return (input_grad, mask_grad)
```

```python
import functools
import math

import jax
import jax.numpy as jnp
from jax import lax
from jax.experimental import pallas as pl
from jax.experimental.pallas import tpu as pltpu
from jax.sharding import PartitionSpec as P

DH = 128
NEG_FILL = -1e30


def contract(left, right, left_dim, right_dim):
    return lax.dot_general(
        left, right, (((left_dim,), (right_dim,)), ((), ())), preferred_element_type=jnp.float32
    )


def attention_kernel(
    per_group, scale_ref, query_ref, grad_ref, key_ref, value_ref, row_seg_ref, key_seg_ref,
    dq_ref, dk_ref, dv_ref, mask_ref,
):
    rows, span = query_ref.shape[0], key_ref.shape[0]
    group = pl.program_id(0)
    score_scale = 1.0 / math.sqrt(DH)
    row_place = lax.broadcasted_iota(jnp.int32, (rows, span), 0) + (span - rows)
    key_place = lax.broadcasted_iota(jnp.int32, (rows, span), 1)
    allowed = (key_place <= row_place) & (key_seg_ref[...] == row_seg_ref[...])
    key, value = key_ref[...], value_ref[...]
    key_total = jnp.zeros((span, DH), jnp.float32)
    value_total = jnp.zeros((span, DH), jnp.float32)
    for j in range(per_group):
        columns = pl.ds(j * DH, DH)
        query = query_ref[:, columns]
        grad = grad_ref[:, columns].astype(jnp.float32)
        scores = jnp.where(allowed, contract(query, key, 1, 1) * score_scale, NEG_FILL)
        row_max = jnp.max(scores, axis=-1, keepdims=True)
        exponent = jnp.exp(scores - row_max)
        inverse = 1.0 / jnp.sum(exponent, axis=-1, keepdims=True)
        head_out = contract(exponent.astype(jnp.bfloat16), value, 1, 0) * inverse
        head_out = head_out.astype(jnp.bfloat16).astype(jnp.float32)
        out_grad = (scale_ref[group * per_group + j] * grad).astype(jnp.bfloat16)
        out_dot = jnp.sum(out_grad.astype(jnp.float32) * head_out, axis=-1, keepdims=True)
        probability = exponent * inverse
        prob_grad = contract(out_grad, value, 1, 1)
        score_grad = (probability * (prob_grad - out_dot)).astype(jnp.bfloat16)
        dq_ref[:, columns] = (contract(score_grad, key, 1, 0) * score_scale).astype(jnp.bfloat16)
        key_total = key_total + contract(score_grad, query, 0, 0)
        value_total = value_total + contract(probability.astype(jnp.bfloat16), out_grad, 0, 0)
        mask_ref[0, pl.ds(j, 1), :] = jnp.sum(head_out * grad, axis=0, keepdims=True)
    dk_ref[...] = (key_total * score_scale).astype(jnp.bfloat16)
    dv_ref[...] = value_total.astype(jnp.bfloat16)


def attention(scale, query, grad, key, value, row_seg, key_seg):
    rows, width = query.shape
    span, narrow = key.shape
    groups = narrow // DH
    per_group = width // narrow
    wide = pl.BlockSpec((rows, per_group * DH), lambda g: (0, g))
    thin = pl.BlockSpec((span, DH), lambda g: (0, g))
    return pl.pallas_call(
        functools.partial(attention_kernel, per_group),
        grid=(groups,),
        in_specs=[
            pl.BlockSpec(memory_space=pltpu.SMEM), wide, wide, thin, thin,
            pl.BlockSpec((rows, 1), lambda g: (0, 0)), pl.BlockSpec((1, span), lambda g: (0, 0)),
        ],
        out_specs=[wide, thin, thin, pl.BlockSpec((1, per_group, DH), lambda g: (g, 0, 0))],
        out_shape=[
            jax.ShapeDtypeStruct((rows, width), jnp.bfloat16),
            jax.ShapeDtypeStruct((span, narrow), jnp.bfloat16),
            jax.ShapeDtypeStruct((span, narrow), jnp.bfloat16),
            jax.ShapeDtypeStruct((groups, per_group, DH), jnp.float32),
        ],
        compiler_params=pltpu.CompilerParams(vmem_limit_bytes=40 * 1024 * 1024),
        cost_estimate=pl.CostEstimate(
            flops=12 * rows * span * width, bytes_accessed=6 * rows * width,
            transcendentals=rows * span * groups * per_group,
        ),
        name="attention",
    )(scale, query, grad, key, value, row_seg, key_seg)


def moved(block, distance):
    count = lax.axis_size("ctx")
    route = [(i, i + distance) for i in range(count) if 0 <= i + distance < count]
    return lax.ppermute(block, "ctx", route)


def swapped(block, flip):
    return lax.ppermute(block, "rep", [(i, i ^ flip) for i in range(lax.axis_size("rep"))])


def half_columns(arrays, half):
    parts = []
    for array in arrays:
        width = array.shape[1] // 2
        parts.append(lax.dynamic_slice_in_dim(array, half * width, width, 1))
    return jnp.concatenate(parts, axis=1)


def in_order(mine, other, place):
    first = place == 0
    return jnp.stack([jnp.where(first, mine, other), jnp.where(first, other, mine)])


def on_device(
    queries, keys, values, grad_out, segment_ids, head_mask, ablated_heads, w_query, w_key, w_value
):
    rows_dev = queries.shape[1]
    local_heads = head_mask.shape[0]
    block_count = lax.axis_size("ctx")
    my_block = lax.axis_index("ctx")
    rep_count, rep = lax.axis_size("rep"), lax.axis_index("rep")
    high, low = rep // 2, rep % 2
    seq_len = block_count * rows_dev
    narrow = keys.shape[2]
    before = min(block_count - 1, (seq_len // 2 + rows_dev - 2) // rows_dev)
    span = (before + 1) * rows_dev

    key_value = jnp.concatenate([keys[0], values[0]], axis=1)
    window = [moved(key_value, d) for d in range(before, 0, -1)] + [key_value]
    window = jnp.concatenate(window, axis=0)
    padded = jnp.concatenate(
        [jnp.full((before * rows_dev,), -1, jnp.int32), segment_ids[0]], axis=0
    )
    key_seg = lax.dynamic_slice_in_dim(padded, my_block * rows_dev, span, 0)
    row_seg = key_seg[before * rows_dev :]

    weights = (w_query, w_key, w_value)
    weight_mine = half_columns(weights, high)
    weight_other = swapped(half_columns(weights, 1 - high), 2)
    weight_pair = in_order(weight_mine, weight_other, high)
    weight_far = swapped(weight_pair, 1)

    head_ids = lax.axis_index("head") * local_heads + jnp.arange(local_heads, dtype=jnp.int32)
    ablate = jnp.any(head_ids[:, None] == ablated_heads[None, :], axis=1)
    head_scale = jnp.where(ablate, 0.0, head_mask)
    dq, dk, dv, mask_rows = attention(
        head_scale, queries[0], grad_out[0], window[:, :narrow], window[:, narrow:],
        row_seg[:, None], key_seg[None, :],
    )
    mask_terms = jnp.sum(mask_rows, axis=2).reshape(local_heads)
    mask_grad = lax.psum(mask_terms, ("ctx", "rep")) / math.sqrt(rep_count * seq_len)

    pair = jnp.concatenate([dk, dv], axis=1)
    total = pair[before * rows_dev :].astype(jnp.float32)
    for d in range(1, before + 1):
        piece = pair[(before - d) * rows_dev : (before - d + 1) * rows_dev]
        total = total + moved(piece, -d).astype(jnp.float32)
    total = total.astype(jnp.bfloat16)
    grads = (dq, total[:, :narrow], total[:, narrow:])
    grad_mine = half_columns(grads, high)
    grad_other = swapped(half_columns(grads, 1 - high), 2)
    grad_pair = in_order(grad_mine, grad_other, high)
    tokens = lax.all_gather(grad_pair, "ctx", axis=1, tiled=True)
    tokens = tokens.reshape(2 * seq_len, -1)
    weight_all = jnp.stack([
        jnp.where(low == 0, weight_pair, weight_far), jnp.where(low == 0, weight_far, weight_pair)
    ], axis=1)
    weight_all = weight_all.reshape(-1, weight_all.shape[-1])
    partial = contract(tokens, weight_all, 1, 1).astype(jnp.bfloat16)
    heads_count = lax.axis_size("head")
    head = lax.axis_index("head")
    partial = partial.reshape(2, seq_len, heads_count, -1)

    def piece_for(prompt, column):
        taken = lax.dynamic_slice_in_dim(partial, prompt, 1, 0)
        return lax.dynamic_slice_in_dim(taken, column, 1, 2)[0, :, 0]

    result = piece_for(high, head).astype(jnp.float32)
    for flip in range(2):
        for shift in range(heads_count):
            if flip == 0 and shift == 0:
                continue
            route = []
            for h in range(heads_count):
                for r in range(rep_count):
                    target = ((h + shift) % heads_count) * rep_count + (r ^ (2 * flip))
                    route.append((h * rep_count + r, target))
            sent = piece_for(high ^ flip, (head + shift) % heads_count)
            result = result + lax.ppermute(sent, ("head", "rep"), route).astype(jnp.float32)
    return (result.astype(jnp.bfloat16)[None], mask_grad)


def solution(mesh):
    placed = (
        P("rep", "ctx", "head"),
        P("rep", "ctx", "head"),
        P("rep", "ctx", "head"),
        P("rep", "ctx", "head"),
        P("rep", None),
        P("head"),
        P(),
        P(("ctx", "rep"), "head"),
        P(("ctx", "rep"), "head"),
        P(("ctx", "rep"), "head"),
    )
    return jax.shard_map(
        on_device,
        mesh=mesh,
        in_specs=placed,
        out_specs=(P("rep", None, ("ctx", "head")), P("head")),
        check_vma=False,
    )
```

```python
import functools
import math

import jax
import jax.numpy as jnp
from jax import lax
from jax.experimental import pallas as pl
from jax.experimental.pallas import tpu as pltpu
from jax.sharding import PartitionSpec as P

DH = 128
NEG_FILL = -1e30


def contract(left, right, left_dim, right_dim):
    return lax.dot_general(
        left, right, (((left_dim,), (right_dim,)), ((), ())), preferred_element_type=jnp.float32
    )


def attention_kernel(
    per_group, scale_ref, query_ref, grad_ref, key_ref, value_ref, row_seg_ref, key_seg_ref,
    dq_ref, dk_ref, dv_ref, mask_ref,
):
    rows, span = query_ref.shape[0], key_ref.shape[0]
    group = pl.program_id(0)
    score_scale = 1.0 / math.sqrt(DH)
    row_place = lax.broadcasted_iota(jnp.int32, (rows, span), 0) + (span - rows)
    key_place = lax.broadcasted_iota(jnp.int32, (rows, span), 1)
    allowed = (key_place <= row_place) & (key_seg_ref[...] == row_seg_ref[...])
    key, value = key_ref[...], value_ref[...]
    key_total = jnp.zeros((span, DH), jnp.float32)
    value_total = jnp.zeros((span, DH), jnp.float32)
    for j in range(per_group):
        columns = pl.ds(j * DH, DH)
        query = query_ref[:, columns]
        grad = grad_ref[:, columns].astype(jnp.float32)
        scores = jnp.where(allowed, contract(query, key, 1, 1) * score_scale, NEG_FILL)
        row_max = jnp.max(scores, axis=-1, keepdims=True)
        exponent = jnp.exp(scores - row_max)
        inverse = 1.0 / jnp.sum(exponent, axis=-1, keepdims=True)
        head_out = contract(exponent.astype(jnp.bfloat16), value, 1, 0) * inverse
        head_out = head_out.astype(jnp.bfloat16).astype(jnp.float32)
        out_grad = (scale_ref[group * per_group + j] * grad).astype(jnp.bfloat16)
        out_dot = jnp.sum(out_grad.astype(jnp.float32) * head_out, axis=-1, keepdims=True)
        probability = exponent * inverse
        prob_grad = contract(out_grad, value, 1, 1)
        score_grad = (probability * (prob_grad - out_dot)).astype(jnp.bfloat16)
        dq_ref[:, columns] = (contract(score_grad, key, 1, 0) * score_scale).astype(jnp.bfloat16)
        key_total = key_total + contract(score_grad, query, 0, 0)
        value_total = value_total + contract(probability.astype(jnp.bfloat16), out_grad, 0, 0)
        mask_ref[0, pl.ds(j, 1), :] = jnp.sum(head_out * grad, axis=0, keepdims=True)
    dk_ref[...] = (key_total * score_scale).astype(jnp.bfloat16)
    dv_ref[...] = value_total.astype(jnp.bfloat16)


def attention(scale, query, grad, key, value, row_seg, key_seg):
    rows, width = query.shape
    span, narrow = key.shape
    groups = narrow // DH
    per_group = width // narrow
    wide = pl.BlockSpec((rows, per_group * DH), lambda g: (0, g))
    thin = pl.BlockSpec((span, DH), lambda g: (0, g))
    return pl.pallas_call(
        functools.partial(attention_kernel, per_group),
        grid=(groups,),
        in_specs=[
            pl.BlockSpec(memory_space=pltpu.SMEM), wide, wide, thin, thin,
            pl.BlockSpec((rows, 1), lambda g: (0, 0)), pl.BlockSpec((1, span), lambda g: (0, 0)),
        ],
        out_specs=[wide, thin, thin, pl.BlockSpec((1, per_group, DH), lambda g: (g, 0, 0))],
        out_shape=[
            jax.ShapeDtypeStruct((rows, width), jnp.bfloat16),
            jax.ShapeDtypeStruct((span, narrow), jnp.bfloat16),
            jax.ShapeDtypeStruct((span, narrow), jnp.bfloat16),
            jax.ShapeDtypeStruct((groups, per_group, DH), jnp.float32),
        ],
        compiler_params=pltpu.CompilerParams(vmem_limit_bytes=40 * 1024 * 1024),
        cost_estimate=pl.CostEstimate(
            flops=12 * rows * span * width, bytes_accessed=6 * rows * width,
            transcendentals=rows * span * groups * per_group,
        ),
        name="attention",
    )(scale, query, grad, key, value, row_seg, key_seg)


def project_kernel(
    mine_ref, other_ref, w0_ref, w1_ref, w2_ref, out_ref,
    tokens, weights, sending, landing, own, local_sem, unit_send, unit_recv, part_send, part_recv,
):
    count, rows = tokens.shape[0], tokens.shape[2]
    width = weights.shape[2]
    mesh_id = pl.DeviceIdType.MESH
    z, x, rep = lax.axis_index("ctx"), lax.axis_index("head"), lax.axis_index("rep")
    y, k = rep // 2, rep % 2
    peers = [
        {"head": 1 - x},
        {"rep": (1 - y) * 2 + k},
        {"head": 1 - x, "rep": (1 - y) * 2 + k},
        {"rep": y * 2 + 1 - k},
    ]
    has_left, has_right = z > 0, z < count - 1

    local = [pltpu.make_async_copy(mine_ref, tokens.at[z, y], local_sem.at[0])]
    places = ((y, k), (1 - y, k), (y, 1 - k))
    for i, (ref, (high, low)) in enumerate(zip((w0_ref, w1_ref, w2_ref), places)):
        local.append(pltpu.make_async_copy(ref, weights.at[high, low], local_sem.at[1 + i]))
    for copy in local:
        copy.start()

    barrier = pltpu.get_barrier_semaphore()
    for peer in peers:
        pl.semaphore_signal(barrier, inc=1, device_id=peer, device_id_type=mesh_id)

    @pl.when(has_left)
    def _():
        pl.semaphore_signal(barrier, inc=1, device_id={"ctx": z - 1}, device_id_type=mesh_id)

    @pl.when(has_right)
    def _():
        pl.semaphore_signal(barrier, inc=1, device_id={"ctx": z + 1}, device_id_type=mesh_id)

    pl.semaphore_wait(barrier, 4 + jnp.minimum(z, 1) + jnp.minimum(count - 1 - z, 1))

    def across():
        return pltpu.make_async_remote_copy(
            src_ref=other_ref, dst_ref=tokens.at[z, y], send_sem=local_sem.at[5],
            recv_sem=unit_recv.at[z, y], device_id=peers[1], device_id_type=mesh_id,
        )

    def along(b, p, side):
        return pltpu.make_async_remote_copy(
            src_ref=tokens.at[b, p], dst_ref=tokens.at[b, p], send_sem=unit_send.at[side, b, p],
            recv_sem=unit_recv.at[b, p], device_id={"ctx": z + (2 * side - 1)},
            device_id_type=mesh_id,
        )

    def part(kind, b):
        return pltpu.make_async_remote_copy(
            src_ref=sending.at[kind - 1, b], dst_ref=landing.at[kind - 1, b],
            send_sem=part_send.at[kind - 1, b], recv_sem=part_recv.at[kind - 1, b],
            device_id=peers[kind - 1], device_id_type=mesh_id,
        )

    def beside(low):
        return pltpu.make_async_remote_copy(
            src_ref=w1_ref, dst_ref=weights.at[1 - y, low], send_sem=local_sem.at[4],
            recv_sem=local_sem.at[6], device_id=peers[3], device_id_type=mesh_id,
        )

    across().start()
    beside(k).start()
    local[0].wait()

    def product(b, p, dx, low):
        high = x if dx == 0 else 1 - x
        return contract(tokens[b, p], weights[high, low], 1, 1)

    def visit(t, carried):
        step, second, side = t // 4, (t // 2) % 2, t % 2
        b = z + step * (2 * side - 1)
        p = y + second * (1 - 2 * y)
        valid = (b >= 0) & (b < count) & ((step > 0) | (side == 0))

        @pl.when(valid)
        def _():
            @pl.when((step > 0) | (second == 1))
            def _():
                along(b, p, 0).wait_recv()

            @pl.when(has_left & ((side == 1) | (step == 0)))
            def _():
                along(b, p, 0).start()

            @pl.when(has_right & (side == 0))
            def _():
                along(b, p, 1).start()

            @pl.when(t == 0)
            def _():
                for copy in local[1:]:
                    copy.wait()
                beside(1 - k).wait_recv()

            for low in range(2):
                sending[second * 2, b, :, low * width : (low + 1) * width] = product(
                    b, p, 1, low
                ).astype(jnp.bfloat16)

            for low in range(2):
                value = product(b, p, 0, low)

                @pl.when(second == 0)
                def _():
                    own[b, :, low * width : (low + 1) * width] = value

                @pl.when(second == 1)
                def _():
                    sending[1, b, :, low * width : (low + 1) * width] = value.astype(jnp.bfloat16)

            @pl.when(second == 0)
            def _():
                part(1, b).start()

            @pl.when(second == 1)
            def _():
                part(3, b).start()
                part(2, b).start()

        return carried

    lax.fori_loop(0, 4 * count, visit, 0)

    def finish(b, carried):
        for kind in (1, 2, 3):
            part(kind, b).wait()
        total = own[b]
        for kind in (1, 2, 3):
            total = total + landing[kind - 1, b].astype(jnp.float32)
        out_ref[pl.ds(pl.multiple_of(b * rows, rows), rows), :] = total.astype(jnp.bfloat16)
        for second in range(2):

            @pl.when(has_left & (b >= z))
            def _():
                along(b, second, 0).wait_send()

            @pl.when(has_right & (b <= z))
            def _():
                along(b, second, 1).wait_send()

        return carried

    lax.fori_loop(0, count, finish, 0)
    across().wait_send()
    beside(k).wait_send()


def project(mine, other, weights, count):
    rows, depth = mine.shape
    width = weights[0].shape[0]
    bf16 = jnp.bfloat16
    dma = pltpu.SemaphoreType.DMA
    vmem = pl.BlockSpec(memory_space=pltpu.VMEM)
    return pl.pallas_call(
        project_kernel,
        in_specs=[vmem, vmem] + [pl.BlockSpec(memory_space=pl.ANY)] * 3,
        out_specs=vmem,
        out_shape=jax.ShapeDtypeStruct((count * rows, 2 * width), bf16),
        scratch_shapes=[
            pltpu.VMEM((count, 2, rows, depth), bf16),
            pltpu.VMEM((2, 2, width, depth), bf16),
            pltpu.VMEM((3, count, rows, 2 * width), bf16),
            pltpu.VMEM((3, count, rows, 2 * width), bf16),
            pltpu.VMEM((count, rows, 2 * width), jnp.float32),
            dma((7,)), dma((2, count, 2)), dma((count, 2)), dma((3, count)), dma((3, count)),
        ],
        compiler_params=pltpu.CompilerParams(
            collective_id=0, has_side_effects=True, vmem_limit_bytes=50 * 1024 * 1024
        ),
        cost_estimate=pl.CostEstimate(
            flops=2 * count * 2 * rows * depth * 4 * width,
            bytes_accessed=2 * 4 * width * depth, transcendentals=0,
        ),
        name="project",
    )(mine, other, *weights)


def moved(block, distance):
    count = lax.axis_size("ctx")
    route = [(i, i + distance) for i in range(count) if 0 <= i + distance < count]
    return lax.ppermute(block, "ctx", route)


def swapped(block, flip):
    return lax.ppermute(block, "rep", [(i, i ^ flip) for i in range(lax.axis_size("rep"))])


def half_columns(arrays, half):
    parts = []
    for array in arrays:
        width = array.shape[1] // 2
        parts.append(lax.dynamic_slice_in_dim(array, half * width, width, 1))
    return jnp.concatenate(parts, axis=1)


def in_order(mine, other, place):
    first = place == 0
    return jnp.stack([jnp.where(first, mine, other), jnp.where(first, other, mine)])


def on_device(
    queries, keys, values, grad_out, segment_ids, head_mask, ablated_heads, w_query, w_key, w_value
):
    rows_dev = queries.shape[1]
    local_heads = head_mask.shape[0]
    block_count = lax.axis_size("ctx")
    my_block = lax.axis_index("ctx")
    rep_count, rep = lax.axis_size("rep"), lax.axis_index("rep")
    high, low = rep // 2, rep % 2
    seq_len = block_count * rows_dev
    narrow = keys.shape[2]
    before = min(block_count - 1, (seq_len // 2 + rows_dev - 2) // rows_dev)
    span = (before + 1) * rows_dev

    key_value = jnp.concatenate([keys[0], values[0]], axis=1)
    window = [moved(key_value, d) for d in range(before, 0, -1)] + [key_value]
    window = jnp.concatenate(window, axis=0)
    padded = jnp.concatenate(
        [jnp.full((before * rows_dev,), -1, jnp.int32), segment_ids[0]], axis=0
    )
    key_seg = lax.dynamic_slice_in_dim(padded, my_block * rows_dev, span, 0)
    row_seg = key_seg[before * rows_dev :]

    weights = (w_query, w_key, w_value)
    weight_mine = half_columns(weights, high)
    weight_other = swapped(half_columns(weights, 1 - high), 2)
    far_mine = swapped(weight_mine, 1)

    head_ids = lax.axis_index("head") * local_heads + jnp.arange(local_heads, dtype=jnp.int32)
    ablate = jnp.any(head_ids[:, None] == ablated_heads[None, :], axis=1)
    head_scale = jnp.where(ablate, 0.0, head_mask)
    dq, dk, dv, mask_rows = attention(
        head_scale, queries[0], grad_out[0], window[:, :narrow], window[:, narrow:],
        row_seg[:, None], key_seg[None, :],
    )
    mask_terms = jnp.sum(mask_rows, axis=2).reshape(local_heads)
    mask_grad = lax.psum(mask_terms, ("ctx", "rep")) / math.sqrt(rep_count * seq_len)

    pair = jnp.concatenate([dk, dv], axis=1)
    total = pair[before * rows_dev :].astype(jnp.float32)
    for d in range(1, before + 1):
        piece = pair[(before - d) * rows_dev : (before - d + 1) * rows_dev]
        total = total + moved(piece, -d).astype(jnp.float32)
    total = total.astype(jnp.bfloat16)
    grads = (dq, total[:, :narrow], total[:, narrow:])
    grad_mine = half_columns(grads, high)
    grad_other = half_columns(grads, 1 - high)
    if lax.axis_size("head") == 2 and rep_count == 4:
        pieces = (weight_mine, weight_other, far_mine)
        result = project(grad_mine, grad_other, pieces, block_count)
        return (result[None], mask_grad)

    grad_other = swapped(grad_other, 2)
    weight_pair = in_order(weight_mine, weight_other, high)
    weight_far = in_order(far_mine, swapped(weight_other, 1), high)
    grad_pair = in_order(grad_mine, grad_other, high)
    tokens = lax.all_gather(grad_pair, "ctx", axis=1, tiled=True)
    tokens = tokens.reshape(2 * seq_len, -1)
    weight_all = jnp.stack([
        jnp.where(low == 0, weight_pair, weight_far), jnp.where(low == 0, weight_far, weight_pair)
    ], axis=1)
    weight_all = weight_all.reshape(-1, weight_all.shape[-1])
    partial = contract(tokens, weight_all, 1, 1).astype(jnp.bfloat16)
    heads_count = lax.axis_size("head")
    head = lax.axis_index("head")
    partial = partial.reshape(2, seq_len, heads_count, -1)

    def piece_for(prompt, column):
        taken = lax.dynamic_slice_in_dim(partial, prompt, 1, 0)
        return lax.dynamic_slice_in_dim(taken, column, 1, 2)[0, :, 0]

    result = piece_for(high, head).astype(jnp.float32)
    for flip in range(2):
        for shift in range(heads_count):
            if flip == 0 and shift == 0:
                continue
            route = []
            for h in range(heads_count):
                for r in range(rep_count):
                    target = ((h + shift) % heads_count) * rep_count + (r ^ (2 * flip))
                    route.append((h * rep_count + r, target))
            sent = piece_for(high ^ flip, (head + shift) % heads_count)
            result = result + lax.ppermute(sent, ("head", "rep"), route).astype(jnp.float32)
    return (result.astype(jnp.bfloat16)[None], mask_grad)


def solution(mesh):
    placed = (
        P("rep", "ctx", "head"),
        P("rep", "ctx", "head"),
        P("rep", "ctx", "head"),
        P("rep", "ctx", "head"),
        P("rep", None),
        P("head"),
        P(),
        P(("ctx", "rep"), "head"),
        P(("ctx", "rep"), "head"),
        P(("ctx", "rep"), "head"),
    )
    return jax.shard_map(
        on_device,
        mesh=mesh,
        in_specs=placed,
        out_specs=(P("rep", None, ("ctx", "head")), P("head")),
        check_vma=False,
    )
```

```python
import functools
import math

import jax
import jax.numpy as jnp
from jax import lax
from jax.experimental import pallas as pl
from jax.experimental.pallas import tpu as pltpu
from jax.sharding import PartitionSpec as P

DH = 128
NEG_FILL = -1e30


def contract(left, right, left_dim, right_dim):
    return lax.dot_general(
        left, right, (((left_dim,), (right_dim,)), ((), ())), preferred_element_type=jnp.float32
    )


def attention_kernel(
    per_group, scale_ref, query_ref, grad_ref, key_ref, value_ref, row_seg_ref, key_seg_ref,
    dq_ref, dk_ref, dv_ref, mask_ref,
):
    rows, span = query_ref.shape[0], key_ref.shape[0]
    group = pl.program_id(0)
    score_scale = 1.0 / math.sqrt(DH)
    row_place = lax.broadcasted_iota(jnp.int32, (rows, span), 0) + (span - rows)
    key_place = lax.broadcasted_iota(jnp.int32, (rows, span), 1)
    allowed = (key_place <= row_place) & (key_seg_ref[...] == row_seg_ref[...])
    key, value = key_ref[...], value_ref[...]
    key_total = jnp.zeros((span, DH), jnp.float32)
    value_total = jnp.zeros((span, DH), jnp.float32)
    for j in range(per_group):
        columns = pl.ds(j * DH, DH)
        query = query_ref[:, columns]
        grad = grad_ref[:, columns].astype(jnp.float32)
        scores = jnp.where(allowed, contract(query, key, 1, 1) * score_scale, NEG_FILL)
        row_max = jnp.max(scores, axis=-1, keepdims=True)
        exponent = jnp.exp(scores - row_max)
        inverse = 1.0 / jnp.sum(exponent, axis=-1, keepdims=True)
        head_out = contract(exponent.astype(jnp.bfloat16), value, 1, 0) * inverse
        head_out = head_out.astype(jnp.bfloat16).astype(jnp.float32)
        out_grad = (scale_ref[group * per_group + j] * grad).astype(jnp.bfloat16)
        out_dot = jnp.sum(out_grad.astype(jnp.float32) * head_out, axis=-1, keepdims=True)
        probability = exponent * inverse
        prob_grad = contract(out_grad, value, 1, 1)
        score_grad = (probability * (prob_grad - out_dot)).astype(jnp.bfloat16)
        dq_ref[:, columns] = (contract(score_grad, key, 1, 0) * score_scale).astype(jnp.bfloat16)
        key_total = key_total + contract(score_grad, query, 0, 0)
        value_total = value_total + contract(probability.astype(jnp.bfloat16), out_grad, 0, 0)
        mask_ref[0, pl.ds(j, 1), :] = jnp.sum(head_out * grad, axis=0, keepdims=True)
    dk_ref[...] = (key_total * score_scale).astype(jnp.bfloat16)
    dv_ref[...] = value_total.astype(jnp.bfloat16)


def attention(scale, query, grad, key, value, row_seg, key_seg):
    rows, width = query.shape
    span, narrow = key.shape
    groups = narrow // DH
    per_group = width // narrow
    wide = pl.BlockSpec((rows, per_group * DH), lambda g: (0, g))
    thin = pl.BlockSpec((span, DH), lambda g: (0, g))
    return pl.pallas_call(
        functools.partial(attention_kernel, per_group),
        grid=(groups,),
        in_specs=[
            pl.BlockSpec(memory_space=pltpu.SMEM), wide, wide, thin, thin,
            pl.BlockSpec((rows, 1), lambda g: (0, 0)), pl.BlockSpec((1, span), lambda g: (0, 0)),
        ],
        out_specs=[wide, thin, thin, pl.BlockSpec((1, per_group, DH), lambda g: (g, 0, 0))],
        out_shape=[
            jax.ShapeDtypeStruct((rows, width), jnp.bfloat16),
            jax.ShapeDtypeStruct((span, narrow), jnp.bfloat16),
            jax.ShapeDtypeStruct((span, narrow), jnp.bfloat16),
            jax.ShapeDtypeStruct((groups, per_group, DH), jnp.float32),
        ],
        compiler_params=pltpu.CompilerParams(vmem_limit_bytes=40 * 1024 * 1024),
        cost_estimate=pl.CostEstimate(
            flops=12 * rows * span * width, bytes_accessed=6 * rows * width,
            transcendentals=rows * span * groups * per_group,
        ),
        name="attention",
    )(scale, query, grad, key, value, row_seg, key_seg)


def project_kernel(
    mine_ref, other_ref, term_ref, w0_ref, w1_ref, w2_ref, wx_ref, out_ref, mask_ref,
    tokens, weights, sending, landing, own, terms, sums, local_sem, unit_send, unit_recv,
    part_send, part_recv, term_send, term_recv,
):
    count, rows = tokens.shape[0], tokens.shape[2]
    width = weights.shape[2]
    early = 8
    mesh_id = pl.DeviceIdType.MESH
    z, x, rep = lax.axis_index("ctx"), lax.axis_index("head"), lax.axis_index("rep")
    y, k = rep // 2, rep % 2
    peers = [
        {"head": 1 - x},
        {"rep": (1 - y) * 2 + k},
        {"head": 1 - x, "rep": (1 - y) * 2 + k},
        {"rep": y * 2 + 1 - k},
    ]
    has_left, has_right = z > 0, z < count - 1

    local = [pltpu.make_async_copy(mine_ref, tokens.at[z, y], local_sem.at[0])]
    places = ((y, k), (1 - y, k), (y, 1 - k))
    near = w1_ref.shape[0]
    for i, (ref, (high, low)) in enumerate(zip((w0_ref, w1_ref, w2_ref), places)):
        filled = weights.at[high, low, pl.ds(0, ref.shape[0])]
        local.append(pltpu.make_async_copy(ref, filled, local_sem.at[1 + i]))
    for copy in local:
        copy.start()

    barrier = pltpu.get_barrier_semaphore()
    for peer in peers:
        pl.semaphore_signal(barrier, inc=1, device_id=peer, device_id_type=mesh_id)

    @pl.when(has_left)
    def _():
        pl.semaphore_signal(barrier, inc=1, device_id={"ctx": z - 1}, device_id_type=mesh_id)

    @pl.when(has_right)
    def _():
        pl.semaphore_signal(barrier, inc=1, device_id={"ctx": z + 1}, device_id_type=mesh_id)

    pl.semaphore_wait(barrier, 4 + jnp.minimum(z, 1) + jnp.minimum(count - 1 - z, 1))

    def across():
        return pltpu.make_async_remote_copy(
            src_ref=other_ref, dst_ref=tokens.at[z, y], send_sem=local_sem.at[5],
            recv_sem=unit_recv.at[z, y], device_id=peers[1], device_id_type=mesh_id,
        )

    def across_term():
        return pltpu.make_async_remote_copy(
            src_ref=term_ref, dst_ref=terms.at[z, y], send_sem=local_sem.at[7],
            recv_sem=term_recv.at[z, y], device_id=peers[1], device_id_type=mesh_id,
        )

    def along_term(b, p, side):
        return pltpu.make_async_remote_copy(
            src_ref=terms.at[b, p], dst_ref=terms.at[b, p], send_sem=term_send.at[side, b, p],
            recv_sem=term_recv.at[b, p], device_id={"ctx": z + (2 * side - 1)},
            device_id_type=mesh_id,
        )

    def beside_sum():
        return pltpu.make_async_remote_copy(
            src_ref=sums.at[0], dst_ref=sums.at[1], send_sem=local_sem.at[8],
            recv_sem=local_sem.at[9], device_id=peers[3], device_id_type=mesh_id,
        )

    def rest_across(high):
        return pltpu.make_async_remote_copy(
            src_ref=wx_ref, dst_ref=weights.at[high, k, pl.ds(near, width - near)],
            send_sem=local_sem.at[10], recv_sem=local_sem.at[11], device_id=peers[1],
            device_id_type=mesh_id,
        )

    def rest_beside(low):
        rest = pl.ds(near, width - near)
        return pltpu.make_async_remote_copy(
            src_ref=weights.at[1 - y, k, rest], dst_ref=weights.at[1 - y, low, rest],
            send_sem=local_sem.at[12], recv_sem=local_sem.at[13], device_id=peers[3],
            device_id_type=mesh_id,
        )

    def along(b, p, side):
        return pltpu.make_async_remote_copy(
            src_ref=tokens.at[b, p], dst_ref=tokens.at[b, p], send_sem=unit_send.at[side, b, p],
            recv_sem=unit_recv.at[b, p], device_id={"ctx": z + (2 * side - 1)},
            device_id_type=mesh_id,
        )

    def part(kind, b):
        return pltpu.make_async_remote_copy(
            src_ref=sending.at[kind - 1, b], dst_ref=landing.at[kind - 1, b],
            send_sem=part_send.at[kind - 1, b], recv_sem=part_recv.at[kind - 1, b],
            device_id=peers[kind - 1], device_id_type=mesh_id,
        )

    def beside(low):
        return pltpu.make_async_remote_copy(
            src_ref=w1_ref, dst_ref=weights.at[1 - y, low, pl.ds(0, near)], send_sem=local_sem.at[4],
            recv_sem=local_sem.at[6], device_id=peers[3], device_id_type=mesh_id,
        )

    terms[z, y] = term_ref[...]
    across_term().start()
    across().start()
    rest_across(y).start()
    beside(k).start()
    local[0].wait()

    def product(b, p, dx, low):
        high = x if dx == 0 else 1 - x
        return contract(tokens[b, p], weights[high, low], 1, 1)

    def unit(t):
        step, second, side = t // 4, (t // 2) % 2, t % 2
        b = z + step * (2 * side - 1)
        p = y + second * (1 - 2 * y)
        return step, second, side, b, p, (b >= 0) & (b < count) & ((step > 0) | (side == 0))

    def receive(t, carried):
        step, second, side, b, p, valid = unit(t)

        @pl.when(valid)
        def _():
            @pl.when((step > 0) | (second == 1))
            def _():
                along(b, p, 0).wait_recv()
                along_term(b, p, 0).wait_recv()

            @pl.when(has_left & ((side == 1) | (step == 0)))
            def _():
                along(b, p, 0).start()
                along_term(b, p, 0).start()

            @pl.when(has_right & (side == 0))
            def _():
                along(b, p, 1).start()
                along_term(b, p, 1).start()

        return carried

    def visit(t, carried):
        step, second, side, b, p, valid = unit(t)

        @pl.when(t == 0)
        def _():
            lax.fori_loop(0, early, receive, 0)
            for copy in local[1:]:
                copy.wait()
            beside(1 - k).wait_recv()
            rest_across(1 - y).wait_recv()
            rest_beside(k).start()
            rest_beside(1 - k).wait_recv()

        @pl.when(t >= early)
        def _():
            receive(t, 0)

        @pl.when(valid)
        def _():
            for low in range(2):
                sending[second * 2, b, :, low * width : (low + 1) * width] = product(
                    b, p, 1, low
                ).astype(jnp.bfloat16)

            for low in range(2):
                value = product(b, p, 0, low)

                @pl.when(second == 0)
                def _():
                    own[b, :, low * width : (low + 1) * width] = value

                @pl.when(second == 1)
                def _():
                    sending[1, b, :, low * width : (low + 1) * width] = value.astype(jnp.bfloat16)

            @pl.when(second == 0)
            def _():
                part(1, b).start()

            @pl.when(second == 1)
            def _():
                part(3, b).start()
                part(2, b).start()

        return carried

    lax.fori_loop(0, 4 * count, visit, 0)

    sums[0] = sum(terms[b, p] for b in range(count) for p in range(2))
    beside_sum().start()

    def finish(b, carried):
        for kind in (1, 2, 3):
            part(kind, b).wait()
        total = own[b]
        for kind in (1, 2, 3):
            total = total + landing[kind - 1, b].astype(jnp.float32)
        out_ref[pl.ds(pl.multiple_of(b * rows, rows), rows), :] = total.astype(jnp.bfloat16)
        for second in range(2):

            @pl.when(has_left & (b >= z))
            def _():
                along(b, second, 0).wait_send()
                along_term(b, second, 0).wait_send()

            @pl.when(has_right & (b <= z))
            def _():
                along(b, second, 1).wait_send()
                along_term(b, second, 1).wait_send()

        return carried

    lax.fori_loop(0, count, finish, 0)
    beside_sum().wait()
    mask_ref[...] = sums[0] + sums[1]
    across().wait_send()
    across_term().wait_send()
    beside(k).wait_send()
    rest_across(y).wait_send()
    rest_beside(k).wait_send()


def project(mine, other, term, weights, count):
    rows, depth = mine.shape
    width = weights[0].shape[0]
    bf16 = jnp.bfloat16
    dma = pltpu.SemaphoreType.DMA
    vmem = pl.BlockSpec(memory_space=pltpu.VMEM)
    return pl.pallas_call(
        project_kernel,
        in_specs=[vmem] * 3 + [pl.BlockSpec(memory_space=pl.ANY)] * 4,
        out_specs=[vmem, vmem],
        out_shape=[
            jax.ShapeDtypeStruct((count * rows, 2 * width), bf16),
            jax.ShapeDtypeStruct(term.shape, jnp.float32),
        ],
        scratch_shapes=[
            pltpu.VMEM((count, 2, rows, depth), bf16),
            pltpu.VMEM((2, 2, width, depth), bf16),
            pltpu.VMEM((3, count, rows, 2 * width), bf16),
            pltpu.VMEM((3, count, rows, 2 * width), bf16),
            pltpu.VMEM((count, rows, 2 * width), jnp.float32),
            pltpu.VMEM((count, 2) + term.shape, jnp.float32),
            pltpu.VMEM((2,) + term.shape, jnp.float32),
            dma((14,)), dma((2, count, 2)), dma((count, 2)), dma((3, count)), dma((3, count)),
            dma((2, count, 2)), dma((count, 2)),
        ],
        compiler_params=pltpu.CompilerParams(
            collective_id=0, has_side_effects=True, vmem_limit_bytes=50 * 1024 * 1024
        ),
        cost_estimate=pl.CostEstimate(
            flops=2 * count * 2 * rows * depth * 4 * width,
            bytes_accessed=2 * 4 * width * depth, transcendentals=0,
        ),
        name="project",
    )(mine, other, term, *weights)


def moved(block, distance):
    count = lax.axis_size("ctx")
    route = [(i, i + distance) for i in range(count) if 0 <= i + distance < count]
    return lax.ppermute(block, "ctx", route)


def swapped(block, flip):
    return lax.ppermute(block, "rep", [(i, i ^ flip) for i in range(lax.axis_size("rep"))])


def half_columns(arrays, half):
    parts = []
    for array in arrays:
        width = array.shape[1] // 2
        parts.append(lax.dynamic_slice_in_dim(array, half * width, width, 1))
    return jnp.concatenate(parts, axis=1)


def in_order(mine, other, place):
    first = place == 0
    return jnp.stack([jnp.where(first, mine, other), jnp.where(first, other, mine)])


def on_device(
    queries, keys, values, grad_out, segment_ids, head_mask, ablated_heads, w_query, w_key, w_value
):
    rows_dev = queries.shape[1]
    local_heads = head_mask.shape[0]
    block_count = lax.axis_size("ctx")
    my_block = lax.axis_index("ctx")
    rep_count, rep = lax.axis_size("rep"), lax.axis_index("rep")
    high, low = rep // 2, rep % 2
    seq_len = block_count * rows_dev
    narrow = keys.shape[2]
    before = min(block_count - 1, (seq_len // 2 + rows_dev - 2) // rows_dev)
    span = (before + 1) * rows_dev

    key_value = jnp.concatenate([keys[0], values[0]], axis=1)
    window = [moved(key_value, d) for d in range(before, 0, -1)] + [key_value]
    window = jnp.concatenate(window, axis=0)
    padded = jnp.concatenate(
        [jnp.full((before * rows_dev,), -1, jnp.int32), segment_ids[0]], axis=0
    )
    key_seg = lax.dynamic_slice_in_dim(padded, my_block * rows_dev, span, 0)
    row_seg = key_seg[before * rows_dev :]

    weights = (w_query, w_key, w_value)
    weight_mine = half_columns(weights, high)
    fused = lax.axis_size("head") == 2 and rep_count == 4 and block_count > 1
    weight_sent = half_columns(weights, 1 - high)
    near = weight_sent.shape[0] * 3 // 4 if fused else weight_sent.shape[0]
    weight_other = swapped(weight_sent[:near], 2)
    far_mine = swapped(weight_mine, 1)

    head_ids = lax.axis_index("head") * local_heads + jnp.arange(local_heads, dtype=jnp.int32)
    ablate = jnp.any(head_ids[:, None] == ablated_heads[None, :], axis=1)
    head_scale = jnp.where(ablate, 0.0, head_mask)
    dq, dk, dv, mask_rows = attention(
        head_scale, queries[0], grad_out[0], window[:, :narrow], window[:, narrow:],
        row_seg[:, None], key_seg[None, :],
    )
    mask_terms = jnp.sum(mask_rows, axis=2).reshape(local_heads)
    mask_norm = math.sqrt(rep_count * seq_len)

    pair = jnp.concatenate([dk, dv], axis=1)
    total = pair[before * rows_dev :].astype(jnp.float32)
    for d in range(1, before + 1):
        piece = pair[(before - d) * rows_dev : (before - d + 1) * rows_dev]
        total = total + moved(piece, -d).astype(jnp.float32)
    total = total.astype(jnp.bfloat16)
    grads = (dq, total[:, :narrow], total[:, narrow:])
    grad_mine = half_columns(grads, high)
    grad_other = half_columns(grads, 1 - high)
    if fused:
        pieces = (weight_mine, weight_other, far_mine, weight_sent[near:])
        term = jnp.zeros((8, DH), jnp.float32).at[0, :local_heads].set(mask_terms)
        result, mask_sum = project(grad_mine, grad_other, term, pieces, block_count)
        return (result[None], mask_sum[0, :local_heads] / mask_norm)

    mask_grad = lax.psum(mask_terms, ("ctx", "rep")) / mask_norm

    grad_other = swapped(grad_other, 2)
    weight_pair = in_order(weight_mine, weight_other, high)
    weight_far = in_order(far_mine, swapped(weight_other, 1), high)
    grad_pair = in_order(grad_mine, grad_other, high)
    tokens = lax.all_gather(grad_pair, "ctx", axis=1, tiled=True)
    tokens = tokens.reshape(2 * seq_len, -1)
    weight_all = jnp.stack([
        jnp.where(low == 0, weight_pair, weight_far), jnp.where(low == 0, weight_far, weight_pair)
    ], axis=1)
    weight_all = weight_all.reshape(-1, weight_all.shape[-1])
    partial = contract(tokens, weight_all, 1, 1).astype(jnp.bfloat16)
    heads_count = lax.axis_size("head")
    head = lax.axis_index("head")
    partial = partial.reshape(2, seq_len, heads_count, -1)

    def piece_for(prompt, column):
        taken = lax.dynamic_slice_in_dim(partial, prompt, 1, 0)
        return lax.dynamic_slice_in_dim(taken, column, 1, 2)[0, :, 0]

    result = piece_for(high, head).astype(jnp.float32)
    for flip in range(2):
        for shift in range(heads_count):
            if flip == 0 and shift == 0:
                continue
            route = []
            for h in range(heads_count):
                for r in range(rep_count):
                    target = ((h + shift) % heads_count) * rep_count + (r ^ (2 * flip))
                    route.append((h * rep_count + r, target))
            sent = piece_for(high ^ flip, (head + shift) % heads_count)
            result = result + lax.ppermute(sent, ("head", "rep"), route).astype(jnp.float32)
    return (result.astype(jnp.bfloat16)[None], mask_grad)


def solution(mesh):
    placed = (
        P("rep", "ctx", "head"),
        P("rep", "ctx", "head"),
        P("rep", "ctx", "head"),
        P("rep", "ctx", "head"),
        P("rep", None),
        P("head"),
        P(),
        P(("ctx", "rep"), "head"),
        P(("ctx", "rep"), "head"),
        P(("ctx", "rep"), "head"),
    )
    return jax.shard_map(
        on_device,
        mesh=mesh,
        in_specs=placed,
        out_specs=(P("rep", None, ("ctx", "head")), P("head")),
        check_vma=False,
    )
```
